1024 devices in a mesh: dp: 256 (over z, y_lo, x), space: 4 (over y_hi, core).
Axes of the slice: x: 4, y: 8 (y_hi: 2, y_lo: 4; y = y_hi * 4 + y_lo), z: 16, core: 2. Of those that a mesh axis runs over, the one named last changes fastest.
Arguments:
- features: bfloat16 [256, 12, 48, 3072], P('dp', 'space'), may hold values from -6 to 6
- norm_grad: bfloat16 [256, 12, 48, 3072], P('dp', 'space'), may hold values from -24 to 24
- token_grads: bfloat16 [256, 620, 3072], P('dp', 'space'), may hold values from -6 to 6
- token_place: int32 [256, 12, 48], P('dp', 'space'), may hold values from 0 to 618, as said below
- valid_rows: int32 [256], P('dp'), may hold values from 6 to 12, as said below
- depth_kernel: bfloat16 [7, 7, 3072], replicated, may hold values from -0.875 to 0.875
- depth_bias: float32 [3072], replicated, may hold values from -4 to 4
- norm_gain: float32 [3072], replicated, may hold values from 0.1 to 1.9
Outputs:
- input_grads: bfloat16 [256, 12, 48, 3072], P('dp', 'space')
- param_grads: float32 [52, 3072], P(None, 'dp')
The draws below stay inside these ranges and needn't reach their ends.
Inputs may be any that keep to these rules, and one draw needn't show every extreme that they name: For each image i there is a prefix p_i with 0 <= p_i <= 32 such that token_place[i, r, c] = p_i + r * 49 + c; some image has p_i = 32 and some has p_i = 0. `valid_rows`: some image has all 12 rows valid and some has 6.
All inputs are finite; a program needn't handle non-finite values.
Results may differ from the reference program's by a relative error of at most 0.004.
Values may be sent and summed in bfloat16 or wider, within the bound.
A program may use at most 64 MiB of HBM per device.

```python
import jax
import jax.numpy as jnp
from jax import lax

C = 3072
KERNEL = 7
COLS = 48
IMAGES = 256
ROWS = 12
SEQ = 620
PREFIX = 32


def draw_token_place(key, part):
    key = jax.random.fold_in(key, 11)
    prefix = jax.random.randint(key, (IMAGES,), 0, PREFIX + 1, dtype=jnp.int32)
    prefix = prefix.at[0].set(PREFIX).at[1].set(0)
    row_part = jnp.arange(ROWS, dtype=jnp.int32)[:, None] * (COLS + 1)
    col_part = jnp.arange(COLS, dtype=jnp.int32)[None, :]
    return (prefix[:, None, None] + row_part[None] + col_part[None]).astype(jnp.int32)


def draw_valid_rows(key, part):
    key = jax.random.fold_in(key, 23)
    counts = jax.random.randint(key, (IMAGES,), ROWS // 2, ROWS + 1, dtype=jnp.int32)
    return counts.at[0].set(ROWS).at[1].set(ROWS // 2)


def raised(values, rng, source, target, parts, factor):
    def block_of(position):
        return (jnp.arange(values.shape[position]) // (values.shape[position] // parts)).reshape((-1,) + (1,) * (values.ndim - 1 - position))

    one_side = jax.random.permutation(rng, parts)[block_of(target)]
    second = (block_of(target) + parts // 2) % parts
    return jnp.where((block_of(source) == one_side) | (block_of(source) == second), factor * values, values)


def levels(own_key, shape, cuts, least, largest):
    factor_of = 1.0
    for dim, blocks in cuts:
        draws = jax.random.uniform(jax.random.fold_in(jax.random.fold_in(own_key, 6), dim), (blocks,), jnp.float32, least / len(cuts), largest / len(cuts))
        factor_of = factor_of * jnp.repeat(jnp.exp(draws), shape[dim] // blocks).reshape((-1,) + (1,) * (len(shape) - 1 - dim))
    return factor_of


def scatter_about(stream_key, dims, scale, reach, cuts=(), kind=jnp.bfloat16):
    drawn = jax.random.normal(stream_key, dims, jnp.float32) * scale
    if len(cuts) > 0:
        drawn = levels(stream_key, dims, cuts, -0.22, 0.18) * drawn
    return jnp.clip(drawn, min=-reach, max=reach).astype(kind)


def noise_with(key, extent, scale, most, split, heavy, kind=jnp.bfloat16):
    drawn = scale * jax.random.normal(key, extent, jnp.float32)
    if split:
        drawn = drawn * levels(key, extent, split, -0.22, 0.18)
    return jnp.clip(raised(drawn, jax.random.fold_in(key, 3), *heavy), -most, most).astype(kind)


def setup_inputs(seed: int = 0) -> dict:
    splits = jax.random.split(jax.random.key(seed), 9)
    return {
        "features": scatter_about(splits[0], (IMAGES, ROWS, COLS, C), 1.0, 6.0, ((0, 256), (1, 4))),
        "norm_grad": noise_with(splits[1], (IMAGES, ROWS, COLS, C), 1.0, 24.0, ((0, 256), (1, 4)), (0, 3, 256, 6.0)),
        "token_grads": scatter_about(splits[2], (IMAGES, SEQ, C), 1.0, 6.0, ((0, 256), (1, 4))),
        "token_place": draw_token_place(jax.random.fold_in(splits[8], 71), 0),
        "valid_rows": draw_valid_rows(jax.random.fold_in(splits[8], 71), 0),
        "depth_kernel": scatter_about(splits[5], (KERNEL, KERNEL, C), (KERNEL * KERNEL) ** -0.5, 0.875),
        "depth_bias": scatter_about(splits[6], (C,), 1.0, 4.0, (), jnp.float32),
        "norm_gain": jnp.clip(1.0 + 0.18 * jax.random.normal(splits[7], (C,), jnp.float32), 0.1, 1.9),
    }


def forward_taps(padded, kernel, height, columns):
    total = jnp.zeros((height, columns, padded.shape[-1]), jnp.float32)
    for tap_row in range(KERNEL):
        for tap_col in range(KERNEL):
            total = total + kernel[tap_row, tap_col].astype(jnp.float32) * padded[tap_row:tap_row + height, tap_col:tap_col + columns]
    return total

def transpose_taps(padded, kernel, height, columns):
    margin = KERNEL // 2
    total = jnp.zeros((height, columns, padded.shape[-1]), jnp.float32)
    for tap_row in range(KERNEL):
        for tap_col in range(KERNEL):
            first_row = 2 * margin - tap_row
            first_col = 2 * margin - tap_col
            total = total + kernel[tap_row, tap_col].astype(jnp.float32) * padded[first_row:first_row + height, first_col:first_col + columns]
    return total

def norm_backward(mixed, norm_piece, norm_gain):
    center = lax.optimization_barrier(jnp.mean(mixed, axis=-1, keepdims=True))
    offset = mixed - center
    spread = lax.optimization_barrier(jnp.mean(offset * offset, axis=-1, keepdims=True))
    inverse = lax.rsqrt(spread + 1e-06)
    normed = offset * inverse
    upstream = norm_piece.astype(jnp.float32)
    scaled = upstream * norm_gain
    grad_mixed = inverse * (scaled - lax.optimization_barrier(jnp.mean(scaled, axis=-1, keepdims=True)) - normed * lax.optimization_barrier(jnp.mean(scaled * normed, axis=-1, keepdims=True)))
    return (grad_mixed.astype(jnp.bfloat16), normed, upstream)

def weight_terms(grad_full, padded, normed, upstream, height, columns):
    term_list = []
    for tap_row in range(KERNEL):
        for tap_col in range(KERNEL):
            term_list.append(lax.optimization_barrier(jnp.sum(grad_full * padded[tap_row:tap_row + height, tap_col:tap_col + columns], axis=(0, 1))))
    term_list.append(lax.optimization_barrier(jnp.sum(grad_full, axis=(0, 1))))
    term_list.append(lax.optimization_barrier(jnp.sum(upstream * normed, axis=(0, 1))))
    term_list.append(lax.optimization_barrier(jnp.sum(upstream, axis=(0, 1))))
    return jnp.stack(term_list)

def image_backward(pixels, norm_piece, seq_piece, place_piece, valid_piece, depth_kernel, depth_bias, norm_gain):
    margin = KERNEL // 2
    height, columns = (pixels.shape[0], pixels.shape[1])
    padded = jnp.pad(pixels.astype(jnp.float32), ((margin, margin), (margin, margin), (0, 0)))
    mixed = depth_bias + forward_taps(padded, depth_kernel, height, columns)
    grad_half, normed, upstream = norm_backward(mixed, norm_piece, norm_gain)
    picked = seq_piece[place_piece.reshape(-1)].reshape(height, columns, -1).astype(jnp.float32)
    live_rows = (jnp.arange(height, dtype=jnp.int32) < valid_piece)[:, None, None]
    residual = jnp.where(live_rows, picked, jnp.float32(0.0))
    grad_full = grad_half.astype(jnp.float32)
    grad_padded = jnp.pad(grad_full, ((margin, margin), (margin, margin), (0, 0)))
    input_grad = (residual + transpose_taps(grad_padded, depth_kernel, height, columns)).astype(jnp.bfloat16)
    partial_value = weight_terms(grad_full, padded, normed, upstream, height, columns)
    return (input_grad, partial_value)

def reference(features, norm_grad, token_grads, token_place, valid_rows, depth_kernel, depth_bias, norm_gain):

    def one_image(total, pieces):
        pixels, norm_piece, seq_piece, place_piece, valid_piece = pieces
        input_grad, partial_value = image_backward(pixels, norm_piece, seq_piece, place_piece, valid_piece, depth_kernel, depth_bias, norm_gain)
        return (total + partial_value, input_grad)
    start = jnp.zeros((KERNEL * KERNEL + 3, features.shape[-1]), jnp.float32)
    param_grads, input_grads = lax.scan(one_image, start, (features, norm_grad, token_grads, token_place, valid_rows))
    return (input_grads, param_grads)
```

```python
import functools

import jax
import jax.numpy as jnp
from jax import lax
from jax.experimental import pallas as pl
from jax.experimental.pallas import tpu as pltpu
from jax.sharding import PartitionSpec as P

KERNEL = 7
NX = 4
NY_LO = 4
LANES = 128
SEGS = 8
TAP_ROWS = 56
F32 = jnp.float32
BF16 = jnp.bfloat16


def fused(
    sizes, feat, ngrad, tok, tail, dk, place, valid, bias, gain, out_ig, out_pg,
    f_own, f_sib, f_cross, n_own, t_all, k_raw, g_own, g_sib, g_cross, o_own,
    f3, g3, n3, w8, mixed, resid, onehot, tmp, pacc, pg, ra, rb, sb, rc, sc, rd, sd, pf,
    local_sem, out_sem, fs_s, fs_r, fx_s, fx_r, gs_s, gs_r, gx_s, gx_r, t_s, t_r,
    a_s, a_r, b_s, b_r, c_s, c_r, d_s, d_r, e_s, e_r, h_s, h_r,
):
    nz, ny_lo, nx, nct, rows, cols, seq = sizes
    ny = 2 * ny_lo
    channels = nct * LANES
    segw = cols // SEGS
    wide = segw + KERNEL - 1
    per_y = 64 // ny
    halfct = nct // 2
    dp, s = lax.axis_index("dp"), lax.axis_index("space")
    x = lax.rem(dp, nx)
    y_lo = lax.rem(lax.div(dp, nx), ny_lo)
    z = lax.div(dp, nx * ny_lo)
    core = lax.rem(s, 2)
    y_hi = lax.div(s, 2)
    y = y_hi * ny_lo + y_lo
    m = core * nx + x
    has_cross = (s == 1) | (s == 2)
    no_cross = (s == 0) | (s == 3)

    def flip(i, n):
        return i + core * (n - 1 - 2 * i)

    def dev(z_, y_, x_, core_):
        hi = lax.div(y_, ny_lo)
        return ((z_ * ny_lo + lax.rem(y_, ny_lo)) * nx + x_, hi * 2 + core_)

    sib = (dp, s + 1 - 2 * core)
    cross = (dp, 3 - s)

    def remote(src, dst, ss, rs, device):
        return pltpu.make_async_remote_copy(
            src_ref=src, dst_ref=dst, send_sem=ss, recv_sem=rs,
            device_id=device, device_id_type=pl.DeviceIdType.MESH,
        )

    local = [pltpu.make_async_copy(dk, k_raw, local_sem.at[0])]
    for r in range(rows):
        local.append(pltpu.make_async_copy(feat.at[0, flip(r, rows)], f_own.at[r], local_sem.at[1 + r]))
        local.append(pltpu.make_async_copy(ngrad.at[0, flip(r, rows)], n_own.at[r], local_sem.at[4 + r]))
    local.append(pltpu.make_async_copy(tok.at[0, pl.ds(0, 144)], t_all.at[pl.ds(32, 144)], local_sem.at[7]))
    local.append(pltpu.make_async_copy(tail, t_all.at[pl.ds(176, 32)], local_sem.at[8]))
    for copy in local:
        copy.start()

    barrier = pltpu.get_barrier_semaphore()

    def greet(device):
        pl.semaphore_signal(barrier, inc=1, device_id=device, device_id_type=pl.DeviceIdType.MESH)

    @pl.when(has_cross)
    def _():
        greet(cross)

    for d in range(2 * nx - 1):
        dd = d + 1
        flat = lax.rem(core * nx + x + dd, 2 * nx)
        greet(dev(z, y, lax.rem(flat, nx), lax.div(flat, nx)))
    for d in range(1, ny):
        greet(dev(z, lax.rem(y + d, ny), x, core))
    for d in range(1, nz):
        greet(dev(lax.rem(z + d, nz), y, x, core))
    peers = 2 * nx - 1 + ny - 1 + nz - 1

    @pl.when(has_cross)
    def _():
        pl.semaphore_wait(barrier, peers + 1)

    @pl.when(no_cross)
    def _():
        pl.semaphore_wait(barrier, peers)

    fx = [remote(feat.at[0, flip(r, rows)], f_cross.at[r], fx_s.at[r], fx_r.at[r], cross) for r in range(rows)]
    fs = [remote(feat.at[0, flip(r, rows)], f_sib.at[r], fs_s.at[r], fs_r.at[r], sib) for r in range(rows)]
    t_next = remote(tail, t_all.at[pl.ds(0, 32)], t_s.at[0], t_r.at[0], (dp, s + 1))
    t_prev = remote(tok.at[0, pl.ds(0, 32)], t_all.at[pl.ds(208, 32)], t_s.at[1], t_r.at[1], (dp, s - 1))

    @pl.when(has_cross)
    def _():
        for r in range(rows):
            fx[r].start()

    for r in range(rows):
        fs[r].start()

    @pl.when(s < 3)
    def _():
        t_next.start()

    @pl.when(s > 0)
    def _():
        t_prev.start()

    @pl.when(no_cross)
    def _():
        f_cross[...] = jnp.zeros_like(f_cross)
        g_cross[...] = jnp.zeros_like(g_cross)

    @pl.when(s == 0)
    def _():
        t_all[pl.ds(0, 32), :] = jnp.zeros((32, channels), BF16)

    @pl.when(s == 3)
    def _():
        t_all[pl.ds(208, 32), :] = jnp.zeros((32, channels), BF16)

    tmp[...] = jnp.zeros_like(tmp)

    def lanes(ct):
        return pl.ds(pl.multiple_of(ct * LANES, LANES), LANES)

    def loop(body):
        lax.fori_loop(0, nct, lambda ct, c: (body(ct), c)[1], 0)

    local[0].wait()

    def spread(ct):
        taps = k_raw[:, :, lanes(ct)].astype(F32)
        for a in range(KERNEL):
            for b in range(KERNEL):
                row = pl.multiple_of((flip(a, KERNEL) * KERNEL + b) * 8, 8)
                w8[ct, pl.ds(row, 8), :] = jnp.broadcast_to(taps[a, b][None, :], (8, LANES))

    loop(spread)

    def weight(ct, a, b):
        return w8[ct, pl.ds((a * KERNEL + b) * 8, 8), :][None]

    def widen(src, row, dst, drow, slot):
        def body(ct):
            tmp[slot, pl.ds(8, cols), :] = src[row, :, lanes(ct)].astype(F32)
            for k in range(wide):
                dst[ct, drow, k] = tmp[slot, pl.ds(8 - KERNEL // 2 + k, SEGS, stride=segw), :]
        return body

    def both(*bodies):
        def body(ct):
            for one in bodies:
                one(ct)
        loop(body)

    for copy in local[1:7]:
        copy.wait()

    def stage_grad(ct):
        for r in range(rows):
            tmp[3 + r, pl.ds(8, cols), :] = n_own[r, :, lanes(ct)].astype(F32)
            for k in range(segw):
                n3[ct, r, k] = tmp[3 + r, pl.ds(8 + k, SEGS, stride=segw), :]

    both(*[widen(f_own, r, f3, 3 + r, r) for r in range(rows)], stage_grad)
    for r in range(rows):
        fs[r].wait_recv()
    both(*[widen(f_sib, r, f3, 8 - r, r) for r in range(rows)])

    def conv(ct, acc, source, combos, backward):
        for e in sorted({e for e, _ in combos}):
            line = source[ct, e]
            for r in range(rows):
                if (e, r) not in combos:
                    continue
                for b in range(KERNEL):
                    if backward:
                        acc[r] = acc[r] + weight(ct, KERNEL - 1 - (e - r), KERNEL - 1 - b) * line[b:b + segw]
                    else:
                        acc[r] = acc[r] + weight(ct, e - r, b) * line[b:b + segw]
        return acc

    all_combos = [(e, r) for e in range(rows + 6) for r in range(rows) if 0 <= e - r < KERNEL]
    near = [(e, r) for e, r in all_combos if e >= 3]

    def forward_near(ct):
        start = jnp.broadcast_to(bias[pl.ds(ct, 1), :][None], (segw, SEGS, LANES))
        acc = conv(ct, [start] * rows, f3, near, False)
        for r in range(rows):
            mixed[ct, r] = acc[r]

    loop(forward_near)

    local[7].wait()
    local[8].wait()

    @pl.when(s > 0)
    def _():
        t_next.wait_recv()

    @pl.when(s < 3)
    def _():
        t_prev.wait_recv()

    first = place[0, 0, 0] - s * seq
    held = valid[0] - s * rows
    width = t_all.shape[0]
    lane = lax.broadcasted_iota(jnp.int32, (SEGS, width), 1)
    seg = lax.broadcasted_iota(jnp.int32, (SEGS, width), 0)
    late = jnp.where(lane < 208, lane - 176 + (seq - 32), lane - 208 + seq)
    late = jnp.where(late < 144, -4096, late)
    position = jnp.where(lane < 176, lane - 32, late)
    for r in range(rows):
        row = flip(r, rows)
        base = jnp.where(row < held, first + row * (cols + 1), -8192)
        for k in range(segw):
            hit = position == base + segw * seg + k
            onehot[pl.ds((r * segw + k) * SEGS, SEGS), :] = jnp.where(hit, 1.0, 0.0).astype(F32)

    def pick(ct):
        found = jnp.dot(onehot[...].astype(BF16), t_all[:, lanes(ct)], preferred_element_type=F32)
        resid[ct] = found.reshape(rows, segw, SEGS, LANES)

    loop(pick)

    inv_c = 1.0 / channels
    gx = [remote(g_own.at[r], g_cross.at[r], gx_s.at[r], gx_r.at[r], cross) for r in range(rows)]
    gs = [remote(g_own.at[r], g_sib.at[r], gs_s.at[r], gs_r.at[r], sib) for r in range(rows)]

    def tap_rows(t):
        return pl.ds(t * 8, 8)

    for r in reversed(range(rows)):
        newest = r == rows - 1

        @pl.when(has_cross)
        def _(r=r):
            fx[2 - r].wait_recv()

        def forward_far(ct, r=r):
            widen(f_cross, 2 - r, f3, r, 0)(ct)
            acc = [mixed[ct, i] for i in range(rows)]
            acc = conv(ct, acc, f3, [(e, i) for e, i in all_combos if e == r], False)
            for i in range(r + 1):
                mixed[ct, i] = acc[i]

        loop(forward_far)
        zero = jnp.zeros((segw, SEGS, LANES), F32)

        def sums(ct, carry, r=r):
            total, scaled = carry
            return total + mixed[ct, r], scaled + n3[ct, r] * gain[pl.ds(ct, 1), :][None]

        total, scaled_sum = lax.fori_loop(0, nct, sums, (zero, zero))
        center = jnp.sum(total, axis=-1, keepdims=True) * inv_c
        scaled_mean = jnp.sum(scaled_sum, axis=-1, keepdims=True) * inv_c

        def moments(ct, carry, r=r, center=center):
            square, inner = carry
            offset = mixed[ct, r] - center
            return square + offset * offset, inner + offset * (n3[ct, r] * gain[pl.ds(ct, 1), :][None])

        square, inner = lax.fori_loop(0, nct, moments, (zero, zero))
        inverse = lax.rsqrt(jnp.sum(square, axis=-1, keepdims=True) * inv_c + 1e-06)
        along = jnp.sum(inner, axis=-1, keepdims=True) * inv_c * inverse

        def finish(ct, r=r, newest=newest, center=center, inverse=inverse, scaled_mean=scaled_mean, along=along):
            upstream = n3[ct, r]
            normed = (mixed[ct, r] - center) * inverse
            scaled = upstream * gain[pl.ds(ct, 1), :][None]
            grad = inverse * (scaled - scaled_mean - normed * along)
            grad = grad.astype(BF16).astype(F32)
            for t, value in ((49, grad), (50, upstream * normed), (51, upstream)):
                part = jnp.sum(value, axis=0)
                if not newest:
                    part = part + pacc[ct, tap_rows(t), :]
                pacc[ct, tap_rows(t), :] = part
            for k in range(segw):
                tmp[6, pl.ds(8 + k, SEGS, stride=segw), :] = grad[k]
            g_own[r, :, lanes(ct)] = tmp[6, pl.ds(8, cols), :].astype(BF16)
            for k in range(wide):
                g3[ct, 3 + r, k] = tmp[6, pl.ds(8 - KERNEL // 2 + k, SEGS, stride=segw), :]

        loop(finish)

        @pl.when(has_cross)
        def _(r=r):
            gx[r].start()

        gs[r].start()

        def taps(ct, r=r, newest=newest):
            grad = g3[ct, 3 + r, pl.ds(KERNEL // 2, segw)]
            for a in range(KERNEL):
                line = f3[ct, r + a]
                for b in range(KERNEL):
                    row = pl.ds(pl.multiple_of((flip(a, KERNEL) * KERNEL + b) * 8, 8), 8)
                    part = jnp.sum(grad * line[b:b + segw], axis=0)
                    if not newest:
                        part = part + pacc[ct, row, :]
                    pacc[ct, row, :] = part

        loop(taps)

    def gather_taps(ct):
        pacc[ct, pl.ds(52 * 8, 32), :] = jnp.zeros((32, LANES), F32)
        for t in range(0, TAP_ROWS, 8):
            part = pacc[ct, pl.ds(t * 8, 8, stride=8), :]
            for i in range(1, 8):
                part = part + pacc[ct, pl.ds(t * 8 + i, 8, stride=8), :]
            pg[ct, pl.ds(t, 8), :] = part

    loop(gather_taps)

    used = pl.ds(0, TAP_ROWS)
    send_a = remote(pg.at[pl.ds(halfct * (1 - core), halfct), used], ra, a_s, a_r, sib)
    send_a.start()

    for r in range(rows):
        gs[r].wait_recv()
    both(*[widen(g_sib, r, g3, 8 - r, r) for r in range(rows)])

    def backward_near(ct):
        acc = conv(ct, [resid[ct, r] for r in range(rows)], g3, near, True)
        for r in range(rows):
            mixed[ct, r] = acc[r]

    def span(body, low, high):
        lax.fori_loop(low, high, lambda ct, c: (body(ct), c)[1], 0)

    span(backward_near, 0, nct // 3)
    send_a.wait_recv()

    def add_a(ct):
        pg[halfct * core + ct, used, :] += ra[ct]

    span(add_a, 0, halfct)

    third = halfct // nx
    sends_b = []
    for d in range(1, nx):
        to = lax.rem(x + d, nx)
        sends_b.append(remote(
            pg.at[pl.ds(halfct * core + third * to, third), used], rb.at[d - 1], b_s.at[d - 1], b_r.at[d - 1],
            dev(z, y, to, core),
        ))
    for copy in sends_b:
        copy.start()
    span(backward_near, nct // 3, nct)
    for copy in sends_b:
        copy.wait_recv()
    sb[...] = jnp.zeros_like(sb)
    for i in range(third):
        part = pg[halfct * core + third * x + i, used, :]
        for d in range(nx - 1):
            part = part + rb[d, i]
        sb[i, used, :] = part

    sends_c = []
    for d in range(1, ny):
        to = lax.rem(y + d, ny)
        sends_c.append(remote(
            sb.at[:, pl.ds(pl.multiple_of(per_y * to, per_y), per_y)], rc.at[d - 1], c_s.at[d - 1], c_r.at[d - 1],
            dev(z, to, x, core),
        ))
    for copy in sends_c:
        copy.start()
    for copy in sends_c:
        copy.wait_recv()
    part = sb[:, pl.ds(pl.multiple_of(per_y * y, per_y), per_y), :]
    for d in range(ny - 1):
        part = part + rc[d]
    sc[...] = part

    sends_d = []
    for j in range(2):
        to = 2 * m + j
        slot = lax.rem(z - to + nz - 1, nz)
        sends_d.append(remote(sc.at[pl.ds(j, 2)], rd.at[slot], d_s.at[j], d_r.at[slot], dev(to, y, x, core)))

        @pl.when(z != to)
        def _(j=j):
            sends_d[j].start()

    owner = lax.div(z, 2) == m
    others = lax.div(z, 2) != m
    sends_e = []
    for d in range(1, 2 * nx):
        flat = lax.rem(m + d, 2 * nx)
        sends_e.append(remote(sd, sd, e_s.at[d - 1], e_r, dev(z, y, lax.rem(flat, nx), lax.div(flat, nx))))

    @pl.when(owner)
    def _():
        for d in range(nz - 1):
            remote(sc.at[pl.ds(0, 2)], rd.at[d], d_s.at[0], d_r.at[d], sib).wait_recv()
        part = sc[pl.ds(lax.rem(z, 2), 2)]
        for d in range(nz - 1):
            part = part + rd[d]
        sd[...] = part
        for copy in sends_e:
            copy.start()

    @pl.when(others)
    def _():
        sends_e[0].wait_recv()

    mine = pl.ds(pl.multiple_of(per_y * y, per_y), per_y)
    sends_h = [
        remote(sd, pf.at[:, mine], h_s.at[d - 1], h_r.at[d - 1], dev(z, lax.rem(y + d, ny), x, core))
        for d in range(1, ny)
    ]
    for copy in sends_h:
        copy.start()
    pf[:, mine, :] = sd[...]

    for r in reversed(range(rows)):
        @pl.when(has_cross)
        def _(r=r):
            gx[2 - r].wait_recv()

    def backward_far(ct):
        for e in range(3):
            widen(g_cross, 2 - e, g3, e, e)(ct)
        acc = [mixed[ct, i] for i in range(rows)]
        acc = conv(ct, acc, g3, [(e, i) for e, i in all_combos if e < 3], True)
        for r in range(rows):
            for k in range(segw):
                tmp[3 + r, pl.ds(8 + k, SEGS, stride=segw), :] = acc[r][k]
            o_own[r, :, lanes(ct)] = tmp[3 + r, pl.ds(8, cols), :].astype(BF16)

    loop(backward_far)
    outs = [pltpu.make_async_copy(o_own.at[r], out_ig.at[0, flip(r, rows)], out_sem.at[r]) for r in range(rows)]
    for copy in outs:
        copy.start()
    for copy in sends_h:
        copy.wait_recv()
    out_pg[...] = pf[...]
    for copy in outs:
        copy.wait()

    for r in range(rows):
        fs[r].wait_send()
        gs[r].wait_send()

    @pl.when(has_cross)
    def _():
        for r in range(rows):
            fx[r].wait_send()
            gx[r].wait_send()

    @pl.when(s < 3)
    def _():
        t_next.wait_send()

    @pl.when(s > 0)
    def _():
        t_prev.wait_send()

    send_a.wait_send()
    for copy in sends_b + sends_c + sends_h:
        copy.wait_send()
    for j in range(2):
        @pl.when(z != 2 * m + j)
        def _(j=j):
            sends_d[j].wait_send()

    @pl.when(owner)
    def _():
        for copy in sends_e:
            copy.wait_send()


def body(features, norm_grad, token_grads, token_place, valid_rows, depth_kernel, depth_bias, norm_gain):
    rows, cols, channels = features.shape[1:]
    seq = token_grads.shape[1]
    nct = channels // LANES
    nx, ny_lo = NX, NY_LO
    dp_size = lax.axis_size("dp")
    nz = dp_size // (nx * ny_lo)
    ny = 2 * ny_lo
    per_y = 64 // ny
    segw = cols // SEGS
    wide = segw + KERNEL - 1
    third = nct // 2 // nx
    any_spec = pl.BlockSpec(memory_space=pl.ANY)
    vmem = pl.BlockSpec(memory_space=pltpu.VMEM)
    smem = pl.BlockSpec(memory_space=pltpu.SMEM)
    line = (rows, cols, channels)
    dma = pltpu.SemaphoreType.DMA
    tail = token_grads[0, seq - 32:]
    input_grads, sums = pl.pallas_call(
        functools.partial(fused, (nz, ny_lo, nx, nct, rows, cols, seq)),
        out_shape=(
            jax.ShapeDtypeStruct(features.shape, BF16),
            jax.ShapeDtypeStruct((2, 64, LANES), F32),
        ),
        in_specs=[any_spec] * 5 + [smem] * 2 + [vmem] * 2,
        out_specs=(any_spec, vmem),
        scratch_shapes=[
            pltpu.VMEM(line, BF16),
            pltpu.VMEM(line, BF16),
            pltpu.VMEM(line, BF16),
            pltpu.VMEM(line, BF16),
            pltpu.VMEM((240, channels), BF16),
            pltpu.VMEM(depth_kernel.shape, BF16),
            pltpu.VMEM(line, BF16),
            pltpu.VMEM(line, BF16),
            pltpu.VMEM(line, BF16),
            pltpu.VMEM(line, BF16),
            pltpu.VMEM((nct, rows + 6, wide, SEGS, LANES), F32),
            pltpu.VMEM((nct, rows + 6, wide, SEGS, LANES), F32),
            pltpu.VMEM((nct, rows, segw, SEGS, LANES), F32),
            pltpu.VMEM((nct, KERNEL * KERNEL * 8, LANES), F32),
            pltpu.VMEM((nct, rows, segw, SEGS, LANES), F32),
            pltpu.VMEM((nct, rows, segw, SEGS, LANES), F32),
            pltpu.VMEM((rows * cols, 240), F32),
            pltpu.VMEM((7, 64, LANES), F32),
            pltpu.VMEM((nct, TAP_ROWS * 8, LANES), F32),
            pltpu.VMEM((nct, TAP_ROWS, LANES), F32),
            pltpu.VMEM((nct // 2, TAP_ROWS, LANES), F32),
            pltpu.VMEM((max(nx - 1, 1), third, TAP_ROWS, LANES), F32),
            pltpu.VMEM((third, 64, LANES), F32),
            pltpu.VMEM((ny - 1, third, per_y, LANES), F32),
            pltpu.VMEM((third, per_y, LANES), F32),
            pltpu.VMEM((nz - 1, 2, per_y, LANES), F32),
            pltpu.VMEM((2, per_y, LANES), F32),
            pltpu.VMEM((2, 64, LANES), F32),
            dma((9,)), dma((rows,)),
            dma((rows,)), dma((rows,)), dma((rows,)), dma((rows,)),
            dma((rows,)), dma((rows,)), dma((rows,)), dma((rows,)),
            dma((2,)), dma((2,)),
            dma, dma,
            dma((max(nx - 1, 1),)), dma((max(nx - 1, 1),)),
            dma((ny - 1,)), dma((ny - 1,)),
            dma((2,)), dma((nz - 1,)),
            dma((2 * nx - 1,)), dma,
            dma((ny - 1,)), dma((ny - 1,)),
        ],
        compiler_params=pltpu.CompilerParams(
            collective_id=0, has_side_effects=True, vmem_limit_bytes=60 * 1024 * 1024,
        ),
    )(
        features, norm_grad, token_grads, tail, depth_kernel, token_place, valid_rows,
        depth_bias.reshape(nct, LANES), norm_gain.reshape(nct, LANES),
    )
    index = lax.axis_index("dp")
    count = channels // dp_size
    start = 64 * (index // (nx * ny_lo) % 2) + count * (index % (nx * ny_lo))
    wide_sums = jnp.concatenate([sums[0], sums[1]], axis=1)
    param_grads = lax.dynamic_slice(wide_sums, (0, start), (KERNEL * KERNEL + 3, count))
    return input_grads, param_grads


def solution(mesh):
    placed = (
        P("dp", "space", None, None),
        P("dp", "space", None, None),
        P("dp", "space", None),
        P("dp", "space", None),
        P("dp"),
        P(),
        P(),
        P(),
    )
    return jax.shard_map(
        body,
        mesh=mesh,
        in_specs=placed,
        out_specs=(P("dp", "space", None, None), P(None, "dp")),
        check_vma=False,
    )
```

```python
import functools

import jax
import jax.numpy as jnp
from jax import lax
from jax.experimental import pallas as pl
from jax.experimental.pallas import tpu as pltpu
from jax.sharding import PartitionSpec as P

KERNEL = 7
NX = 4
NY_LO = 4
LANES = 128
SEGS = 8
TAP_ROWS = 56
F32 = jnp.float32
BF16 = jnp.bfloat16


def fused(
    sizes, feat, ngrad, tok, dk, place, valid, bias, gain, out_ig, out_pg,
    f_own, f_sib, f_cross, n_own, t_own, t_tail, t_side, p_own, k_raw, g_own, g_sib, g_cross, o_own,
    f3, g3, n3, w8, mixed, resid, hot_own, hot_side, tmp, pacc, pg, ra, rb, sb, rc, sc, rd, sd, pf,
    local_sem, out_sem, fs_s, fs_r, fx_s, fx_r, gs_s, gs_r, gx_s, gx_r, t_s, t_r,
    a_s, a_r, b_s, b_r, c_s, c_r, d_s, d_r, e_s, e_r, h_s, h_r,
):
    nz, ny_lo, nx, nct, rows, cols, seq = sizes
    ny = 2 * ny_lo
    channels = nct * LANES
    segw = cols // SEGS
    wide = segw + KERNEL - 1
    per_y = 64 // ny
    halfct = nct // 2
    dp, s = lax.axis_index("dp"), lax.axis_index("space")
    x = lax.rem(dp, nx)
    y_lo = lax.rem(lax.div(dp, nx), ny_lo)
    z = lax.div(dp, nx * ny_lo)
    core = lax.rem(s, 2)
    y_hi = lax.div(s, 2)
    y = y_hi * ny_lo + y_lo
    m = core * nx + x
    has_cross = (s == 1) | (s == 2)
    no_cross = (s == 0) | (s == 3)

    def flip(i, n):
        return i + core * (n - 1 - 2 * i)

    def dev(z_, y_, x_, core_):
        hi = lax.div(y_, ny_lo)
        return ((z_ * ny_lo + lax.rem(y_, ny_lo)) * nx + x_, hi * 2 + core_)

    sib = (dp, s + 1 - 2 * core)
    cross = (dp, 3 - s)

    def remote(src, dst, ss, rs, device):
        return pltpu.make_async_remote_copy(
            src_ref=src, dst_ref=dst, send_sem=ss, recv_sem=rs,
            device_id=device, device_id_type=pl.DeviceIdType.MESH,
        )

    local = [pltpu.make_async_copy(dk, k_raw, local_sem.at[0])]
    for r in range(rows):
        local.append(pltpu.make_async_copy(feat.at[0, flip(r, rows)], f_own.at[r], local_sem.at[1 + r]))
        local.append(pltpu.make_async_copy(ngrad.at[0, flip(r, rows)], n_own.at[r], local_sem.at[4 + r]))
    local.append(pltpu.make_async_copy(tok.at[0], t_own, local_sem.at[7]))
    local.append(pltpu.make_async_copy(place, p_own, local_sem.at[8]))
    for copy in local:
        copy.start()

    t_side[...] = jnp.zeros_like(t_side)

    barrier = pltpu.get_barrier_semaphore()

    def greet(device):
        pl.semaphore_signal(barrier, inc=1, device_id=device, device_id_type=pl.DeviceIdType.MESH)

    @pl.when(has_cross)
    def _():
        greet(cross)

    for d in range(2 * nx - 1):
        dd = d + 1
        flat = lax.rem(core * nx + x + dd, 2 * nx)
        greet(dev(z, y, lax.rem(flat, nx), lax.div(flat, nx)))
    for d in range(1, ny):
        greet(dev(z, lax.rem(y + d, ny), x, core))
    for d in range(1, nz):
        greet(dev(lax.rem(z + d, nz), y, x, core))
    peers = 2 * nx - 1 + ny - 1 + nz - 1

    tmp[...] = jnp.zeros_like(tmp)

    def lanes(ct):
        return pl.ds(pl.multiple_of(ct * LANES, LANES), LANES)

    def loop(body):
        lax.fori_loop(0, nct, lambda ct, c: (body(ct), c)[1], 0)

    local[0].wait()

    def spread(ct):
        taps = k_raw[:, :, lanes(ct)].astype(F32)
        for a in range(KERNEL):
            for b in range(KERNEL):
                row = pl.multiple_of((flip(a, KERNEL) * KERNEL + b) * 8, 8)
                w8[ct, pl.ds(row, 8), :] = jnp.broadcast_to(taps[a, b][None, :], (8, LANES))

    loop(spread)

    @pl.when(has_cross)
    def _():
        pl.semaphore_wait(barrier, peers + 1)

    @pl.when(no_cross)
    def _():
        pl.semaphore_wait(barrier, peers)

    fx = [remote(feat.at[0, flip(r, rows)], f_cross.at[r], fx_s.at[r], fx_r.at[r], cross) for r in range(rows)]
    fs = [remote(feat.at[0, flip(r, rows)], f_sib.at[r], fs_s.at[r], fs_r.at[r], sib) for r in range(rows)]
    t_next = remote(t_tail, t_side.at[pl.ds(0, 32)], t_s.at[0], t_r.at[0], sib)
    t_prev = remote(tok.at[0, pl.ds(0, 32)], t_side.at[pl.ds(32, 32)], t_s.at[0], t_r.at[0], sib)
    t_next_x = remote(t_tail.at[pl.ds(16, 16)], t_side.at[pl.ds(16, 16)], t_s.at[1], t_r.at[1], cross)
    t_prev_x = remote(tok.at[0, pl.ds(0, 16)], t_side.at[pl.ds(32, 16)], t_s.at[1], t_r.at[1], cross)

    def send_row(r):
        @pl.when(has_cross)
        def _():
            fx[r].start()

    send_row(0)
    for r in range(rows):
        fs[r].start()

    @pl.when(no_cross)
    def _():
        f_cross[...] = jnp.zeros_like(f_cross)
        g_cross[...] = jnp.zeros_like(g_cross)

    def weight(ct, a, b):
        return w8[ct, pl.ds((a * KERNEL + b) * 8, 8), :][None]

    def widen(src, row, dst, drow, slot):
        def body(ct):
            tmp[slot, pl.ds(8, cols), :] = src[row, :, lanes(ct)].astype(F32)
            for k in range(wide):
                dst[ct, drow, k] = tmp[slot, pl.ds(8 - KERNEL // 2 + k, SEGS, stride=segw), :]
        return body

    def both(*bodies):
        def body(ct):
            for one in bodies:
                one(ct)
        loop(body)

    for copy in local[1:7]:
        copy.wait()

    def stage_grad(ct):
        for r in range(rows):
            tmp[3 + r, pl.ds(8, cols), :] = n_own[r, :, lanes(ct)].astype(F32)
            for k in range(segw):
                n3[ct, r, k] = tmp[3 + r, pl.ds(8 + k, SEGS, stride=segw), :]

    both(*[widen(f_own, r, f3, 3 + r, r) for r in range(rows)], stage_grad)
    send_row(1)
    for r in range(rows):
        fs[r].wait_recv()
    both(*[widen(f_sib, r, f3, 8 - r, r) for r in range(rows)])

    def conv(ct, acc, source, combos, backward):
        for e in sorted({e for e, _ in combos}):
            line = source[ct, e]
            for r in range(rows):
                if (e, r) not in combos:
                    continue
                for b in range(KERNEL):
                    if backward:
                        acc[r] = acc[r] + weight(ct, KERNEL - 1 - (e - r), KERNEL - 1 - b) * line[b:b + segw]
                    else:
                        acc[r] = acc[r] + weight(ct, e - r, b) * line[b:b + segw]
        return acc

    all_combos = [(e, r) for e in range(rows + 6) for r in range(rows) if 0 <= e - r < KERNEL]
    near = [(e, r) for e, r in all_combos if e >= 3]

    def forward_near(ct):
        start = jnp.broadcast_to(bias[pl.ds(ct, 1), :][None], (segw, SEGS, LANES))
        acc = conv(ct, [start] * rows, f3, near, False)
        for r in range(rows):
            mixed[ct, r] = acc[r]

    loop(forward_near)
    send_row(2)

    local[7].wait()
    local[8].wait()
    where_tail = lax.broadcasted_iota(jnp.int32, (32, seq), 1) - lax.broadcasted_iota(jnp.int32, (32, seq), 0)
    tail_rows = jnp.where(where_tail == seq - 32, 1.0, 0.0).astype(BF16)

    group = 6

    def broad(i):
        return pl.ds(pl.multiple_of(i * group * LANES, group * LANES), group * LANES)

    def cut_tail(i, carry):
        found = jnp.dot(tail_rows, t_own[:, broad(i)], preferred_element_type=F32)
        t_tail[:, broad(i)] = found.astype(BF16)
        return carry

    lax.fori_loop(0, nct // group, cut_tail, 0)

    @pl.when(core == 0)
    def _():
        t_next.start()

    @pl.when(core == 1)
    def _():
        t_prev.start()

    @pl.when(s == 1)
    def _():
        t_next_x.start()

    @pl.when(s == 2)
    def _():
        t_prev_x.start()

    def pick_tokens():
        t_next.wait_recv()

        @pl.when(has_cross)
        def _():
            t_next_x.wait_recv()

        first = p_own[0, pl.ds(0, 1), pl.ds(0, 1)] - s * seq
        held = valid[0] - s * rows
        for r in range(rows):
            row = flip(r, rows)
            base = first + jnp.where(row < held, row * (cols + 1), -8192)
            for k in range(segw):
                target = base + k + segw * lax.broadcasted_iota(jnp.int32, (SEGS, 1), 0)
                at = pl.ds((r * segw + k) * SEGS, SEGS)
                lane = lax.broadcasted_iota(jnp.int32, (SEGS, seq), 1)
                hot_own[at, :] = jnp.where(lane == target, 1.0, 0.0).astype(F32)
                lane = lax.broadcasted_iota(jnp.int32, (SEGS, 64), 1)
                lane = jnp.where(lane < 32, lane - 32, lane - 32 + seq)
                hot_side[at, :] = jnp.where(lane == target, 1.0, 0.0).astype(F32)

        def pick(i, carry):
            found = jnp.dot(hot_own[...].astype(BF16), t_own[:, broad(i)], preferred_element_type=F32)
            found += jnp.dot(hot_side[...].astype(BF16), t_side[:, broad(i)], preferred_element_type=F32)
            for j in range(group):
                part = found[:, j * LANES:(j + 1) * LANES]
                resid[i * group + j] = part.reshape(rows, segw, SEGS, LANES)
            return carry

        lax.fori_loop(0, nct // group, pick, 0)

    inv_c = 1.0 / channels
    gx = [remote(g_own.at[r], g_cross.at[r], gx_s.at[r], gx_r.at[r], cross) for r in range(rows)]
    gs = [remote(g_own.at[r], g_sib.at[r], gs_s.at[r], gs_r.at[r], sib) for r in range(rows)]

    def tap_rows(t):
        return pl.ds(t * 8, 8)

    for r in reversed(range(rows)):
        newest = r == rows - 1

        @pl.when(has_cross)
        def _(r=r):
            fx[2 - r].wait_recv()

        def forward_far(ct, r=r):
            widen(f_cross, 2 - r, f3, r, 0)(ct)
            acc = [mixed[ct, i] for i in range(rows)]
            acc = conv(ct, acc, f3, [(e, i) for e, i in all_combos if e == r], False)
            for i in range(r + 1):
                mixed[ct, i] = acc[i]

        loop(forward_far)
        zero = jnp.zeros((segw, SEGS, LANES), F32)

        def sums(ct, carry, r=r):
            total, scaled = carry
            return total + mixed[ct, r], scaled + n3[ct, r] * gain[pl.ds(ct, 1), :][None]

        total, scaled_sum = lax.fori_loop(0, nct, sums, (zero, zero))
        center = jnp.sum(total, axis=-1, keepdims=True) * inv_c
        scaled_mean = jnp.sum(scaled_sum, axis=-1, keepdims=True) * inv_c

        def moments(ct, carry, r=r, center=center):
            square, inner = carry
            offset = mixed[ct, r] - center
            return square + offset * offset, inner + offset * (n3[ct, r] * gain[pl.ds(ct, 1), :][None])

        square, inner = lax.fori_loop(0, nct, moments, (zero, zero))
        inverse = lax.rsqrt(jnp.sum(square, axis=-1, keepdims=True) * inv_c + 1e-06)
        along = jnp.sum(inner, axis=-1, keepdims=True) * inv_c * inverse

        def finish(ct, r=r, newest=newest, center=center, inverse=inverse, scaled_mean=scaled_mean, along=along):
            upstream = n3[ct, r]
            normed = (mixed[ct, r] - center) * inverse
            scaled = upstream * gain[pl.ds(ct, 1), :][None]
            grad = inverse * (scaled - scaled_mean - normed * along)
            grad = grad.astype(BF16).astype(F32)
            for t, value in ((49, grad), (50, upstream * normed), (51, upstream)):
                part = jnp.sum(value, axis=0)
                if not newest:
                    part = part + pacc[ct, tap_rows(t), :]
                pacc[ct, tap_rows(t), :] = part
            for k in range(segw):
                tmp[6, pl.ds(8 + k, SEGS, stride=segw), :] = grad[k]
            g_own[r, :, lanes(ct)] = tmp[6, pl.ds(8, cols), :].astype(BF16)
            for k in range(wide):
                g3[ct, 3 + r, k] = tmp[6, pl.ds(8 - KERNEL // 2 + k, SEGS, stride=segw), :]

        loop(finish)

        if r > 0:
            @pl.when(has_cross)
            def _(r=r):
                gx[r].start()

        gs[r].start()

        def taps(ct, r=r, newest=newest):
            grad = g3[ct, 3 + r, pl.ds(KERNEL // 2, segw)]
            for a in range(KERNEL):
                line = f3[ct, r + a]
                for b in range(KERNEL):
                    row = pl.ds(pl.multiple_of((flip(a, KERNEL) * KERNEL + b) * 8, 8), 8)
                    part = jnp.sum(grad * line[b:b + segw], axis=0)
                    if not newest:
                        part = part + pacc[ct, row, :]
                    pacc[ct, row, :] = part

        if r > 0:
            loop(taps)

    def gather_taps(ct):
        pacc[ct, pl.ds(52 * 8, 32), :] = jnp.zeros((32, LANES), F32)
        for t in range(0, TAP_ROWS, 8):
            part = pacc[ct, pl.ds(t * 8, 8, stride=8), :]
            for i in range(1, 8):
                part = part + pacc[ct, pl.ds(t * 8 + i, 8, stride=8), :]
            pg[ct, pl.ds(t, 8), :] = part

    used = pl.ds(0, TAP_ROWS)
    third = halfct // nx
    sends_a, sends_b = [], []
    for d in range(nx):
        to = lax.rem(x + 1 + d, nx)
        away = halfct * (1 - core) + third * to
        mine = halfct * core + third * to
        sends_a.append(remote(pg.at[pl.ds(away, third), used], ra.at[d], a_s.at[d], a_r.at[d], sib))
        if d < nx - 1:
            sends_b.append(remote(
                pg.at[pl.ds(mine, third), used], rb.at[d], b_s.at[d], b_r.at[d], dev(z, y, to, core),
            ))

    def span(body, low, high):
        lax.fori_loop(low, high, lambda ct, c: (body(ct), c)[1], 0)

    def pass_on(d):
        sends_a[d].wait_recv()
        mine = halfct * core + third * lax.rem(x + 1 + d, nx)
        for i in range(third):
            pg[mine + i, used, :] += ra[d, i]
        if d < nx - 1:
            sends_b[d].start()

    for d in range(nx):
        to = third * lax.rem(x + 1 + d, nx)

        def last_taps(i, to=to):
            other = jnp.where(i < third, 1 - core, core)
            ct = halfct * other + to + lax.rem(i, third)
            taps(ct)
            gather_taps(ct)

        span(last_taps, 0, 2 * third)
        sends_a[d].start()
        if d > 0:
            pass_on(d - 1)
    pass_on(nx - 1)

    for r in range(rows):
        gs[r].wait_recv()
    both(*[widen(g_sib, r, g3, 8 - r, r) for r in range(rows)])

    def backward_near(ct):
        zero = jnp.zeros((segw, SEGS, LANES), F32)
        acc = conv(ct, [zero] * rows, g3, near, True)
        for r in range(rows):
            mixed[ct, r] = acc[r]

    span(backward_near, 0, nct // 4)
    for copy in sends_b:
        copy.wait_recv()
    sb[...] = jnp.zeros_like(sb)
    for i in range(third):
        part = pg[halfct * core + third * x + i, used, :]
        for d in range(nx - 1):
            part = part + rb[d, i]
        sb[i, used, :] = part

    sends_c = []
    for d in range(1, ny):
        to = lax.rem(y + d, ny)
        sends_c.append(remote(
            sb.at[:, pl.ds(pl.multiple_of(per_y * to, per_y), per_y)], rc.at[d - 1], c_s.at[d - 1], c_r.at[d - 1],
            dev(z, to, x, core),
        ))
    for copy in sends_c:
        copy.start()

    @pl.when(has_cross)
    def _():
        gx[0].start()

    span(backward_near, nct // 4, nct // 2)
    for copy in sends_c:
        copy.wait_recv()
    part = sb[:, pl.ds(pl.multiple_of(per_y * y, per_y), per_y), :]
    for d in range(ny - 1):
        part = part + rc[d]
    sc[...] = part

    sends_d = []
    for j in range(2):
        to = 2 * m + j
        slot = lax.rem(z - to + nz - 1, nz)
        sends_d.append(remote(sc.at[pl.ds(j, 2)], rd.at[slot], d_s.at[j], d_r.at[slot], dev(to, y, x, core)))

        @pl.when(z != to)
        def _(j=j):
            sends_d[j].start()

    span(backward_near, nct // 2, 3 * nct // 4)
    owner = lax.div(z, 2) == m
    others = lax.div(z, 2) != m
    sends_e = []
    for d in range(1, 2 * nx):
        flat = lax.rem(m + d, 2 * nx)
        sends_e.append(remote(sd, sd, e_s.at[d - 1], e_r, dev(z, y, lax.rem(flat, nx), lax.div(flat, nx))))

    mine = pl.ds(pl.multiple_of(per_y * y, per_y), per_y)
    sends_h = [
        remote(sd, pf.at[:, mine], h_s.at[d - 1], h_r.at[d - 1], dev(z, lax.rem(y + d, ny), x, core))
        for d in range(1, ny)
    ]

    @pl.when(owner)
    def _():
        for d in range(nz - 1):
            remote(sc.at[pl.ds(0, 2)], rd.at[d], d_s.at[0], d_r.at[d], sib).wait_recv()
        part = sc[pl.ds(lax.rem(z, 2), 2)]
        for d in range(nz - 1):
            part = part + rd[d]
        sd[...] = part
        for copy in sends_e + sends_h:
            copy.start()

    span(backward_near, 3 * nct // 4, nct)
    pick_tokens()

    @pl.when(others)
    def _():
        sends_e[0].wait_recv()
        for copy in sends_h:
            copy.start()

    pf[:, mine, :] = sd[...]

    for r in reversed(range(rows)):
        @pl.when(has_cross)
        def _(r=r):
            gx[2 - r].wait_recv()

    def backward_far(ct):
        for e in range(3):
            widen(g_cross, 2 - e, g3, e, e)(ct)
        acc = [mixed[ct, i] + resid[ct, i] for i in range(rows)]
        acc = conv(ct, acc, g3, [(e, i) for e, i in all_combos if e < 3], True)
        for r in range(rows):
            for k in range(segw):
                tmp[3 + r, pl.ds(8 + k, SEGS, stride=segw), :] = acc[r][k]
            o_own[r, :, lanes(ct)] = tmp[3 + r, pl.ds(8, cols), :].astype(BF16)

    loop(backward_far)
    outs = [pltpu.make_async_copy(o_own.at[r], out_ig.at[0, flip(r, rows)], out_sem.at[r]) for r in range(rows)]
    for copy in outs:
        copy.start()
    for copy in sends_h:
        copy.wait_recv()
    out_pg[:, pl.ds(0, LANES)] = pf[0]
    out_pg[:, pl.ds(LANES, LANES)] = pf[1]
    for copy in outs:
        copy.wait()

    for r in range(rows):
        fs[r].wait_send()
        gs[r].wait_send()

    @pl.when(has_cross)
    def _():
        for r in range(rows):
            fx[r].wait_send()
            gx[r].wait_send()

    @pl.when(core == 0)
    def _():
        t_next.wait_send()

    @pl.when(core == 1)
    def _():
        t_prev.wait_send()

    @pl.when(s == 1)
    def _():
        t_next_x.wait_send()

    @pl.when(s == 2)
    def _():
        t_prev_x.wait_send()

    for copy in sends_a + sends_b + sends_c + sends_h:
        copy.wait_send()
    for j in range(2):
        @pl.when(z != 2 * m + j)
        def _(j=j):
            sends_d[j].wait_send()

    @pl.when(owner)
    def _():
        for copy in sends_e:
            copy.wait_send()


def body(features, norm_grad, token_grads, token_place, valid_rows, depth_kernel, depth_bias, norm_gain):
    rows, cols, channels = features.shape[1:]
    seq = token_grads.shape[1]
    nct = channels // LANES
    nx, ny_lo = NX, NY_LO
    dp_size = lax.axis_size("dp")
    nz = dp_size // (nx * ny_lo)
    ny = 2 * ny_lo
    per_y = 64 // ny
    segw = cols // SEGS
    wide = segw + KERNEL - 1
    third = nct // 2 // nx
    any_spec = pl.BlockSpec(memory_space=pl.ANY)
    vmem = pl.BlockSpec(memory_space=pltpu.VMEM)
    smem = pl.BlockSpec(memory_space=pltpu.SMEM)
    line = (rows, cols, channels)
    dma = pltpu.SemaphoreType.DMA
    input_grads, sums = pl.pallas_call(
        functools.partial(fused, (nz, ny_lo, nx, nct, rows, cols, seq)),
        out_shape=(
            jax.ShapeDtypeStruct(features.shape, BF16),
            jax.ShapeDtypeStruct((64, 2 * LANES), F32),
        ),
        in_specs=[any_spec] * 5 + [smem] + [vmem] * 2,
        out_specs=(any_spec, vmem),
        scratch_shapes=[
            pltpu.VMEM(line, BF16),
            pltpu.VMEM(line, BF16),
            pltpu.VMEM(line, BF16),
            pltpu.VMEM(line, BF16),
            pltpu.VMEM((seq, channels), BF16),
            pltpu.VMEM((32, channels), BF16),
            pltpu.VMEM((64, channels), BF16),
            pltpu.VMEM((rows, 1, cols), jnp.int32),
            pltpu.VMEM(depth_kernel.shape, BF16),
            pltpu.VMEM(line, BF16),
            pltpu.VMEM(line, BF16),
            pltpu.VMEM(line, BF16),
            pltpu.VMEM(line, BF16),
            pltpu.VMEM((nct, rows + 6, wide, SEGS, LANES), F32),
            pltpu.VMEM((nct, rows + 6, wide, SEGS, LANES), F32),
            pltpu.VMEM((nct, rows, segw, SEGS, LANES), F32),
            pltpu.VMEM((nct, KERNEL * KERNEL * 8, LANES), F32),
            pltpu.VMEM((nct, rows, segw, SEGS, LANES), F32),
            pltpu.VMEM((nct, rows, segw, SEGS, LANES), F32),
            pltpu.VMEM((rows * cols, seq), F32),
            pltpu.VMEM((rows * cols, 64), F32),
            pltpu.VMEM((7, 64, LANES), F32),
            pltpu.VMEM((nct, TAP_ROWS * 8 + 64, LANES), F32),
            pltpu.VMEM((nct, TAP_ROWS, LANES), F32),
            pltpu.VMEM((nx, third, TAP_ROWS, LANES), F32),
            pltpu.VMEM((max(nx - 1, 1), third, TAP_ROWS, LANES), F32),
            pltpu.VMEM((third, 64, LANES), F32),
            pltpu.VMEM((ny - 1, third, per_y, LANES), F32),
            pltpu.VMEM((third, per_y, LANES), F32),
            pltpu.VMEM((nz - 1, 2, per_y, LANES), F32),
            pltpu.VMEM((2, per_y, LANES), F32),
            pltpu.VMEM((2, 64, LANES), F32),
            dma((9,)), dma((rows,)),
            dma((rows,)), dma((rows,)), dma((rows,)), dma((rows,)),
            dma((rows,)), dma((rows,)), dma((rows,)), dma((rows,)),
            dma((2,)), dma((2,)),
            dma((nx,)), dma((nx,)),
            dma((max(nx - 1, 1),)), dma((max(nx - 1, 1),)),
            dma((ny - 1,)), dma((ny - 1,)),
            dma((2,)), dma((nz - 1,)),
            dma((2 * nx - 1,)), dma,
            dma((ny - 1,)), dma((ny - 1,)),
        ],
        compiler_params=pltpu.CompilerParams(
            collective_id=0, has_side_effects=True, vmem_limit_bytes=60 * 1024 * 1024,
        ),
    )(
        features, norm_grad, token_grads, depth_kernel, jnp.transpose(token_place, (1, 0, 2)), valid_rows,
        depth_bias.reshape(nct, LANES), norm_gain.reshape(nct, LANES),
    )
    index = lax.axis_index("dp")
    count = channels // dp_size
    start = 64 * (index // (nx * ny_lo) % 2) + count * (index % (nx * ny_lo))
    param_grads = lax.dynamic_slice(sums, (0, start), (KERNEL * KERNEL + 3, count))
    return input_grads, param_grads


def solution(mesh):
    placed = (
        P("dp", "space", None, None),
        P("dp", "space", None, None),
        P("dp", "space", None),
        P("dp", "space", None),
        P("dp"),
        P(),
        P(),
        P(),
    )
    return jax.shard_map(
        body,
        mesh=mesh,
        in_specs=placed,
        out_specs=(P("dp", "space", None, None), P(None, "dp")),
        check_vma=False,
    )
```
